256 devices in a mesh: slab: 32 (over z, y), col: 8 (over x, core).
Axes of the slice: x: 4, y: 4, z: 8, core: 2. Of those that a mesh axis runs over, the one named last changes fastest.
Arguments:
- right_side: float32 [256, 256, 128], P('slab', 'col'), may hold values from -6 to 6
- stencil_weights: float32 [27, 256, 256, 128], P(None, 'slab', 'col'), as said below
- cheb_steps: float32 [6], replicated, may hold values from 0.4 to 1
- send_slot: int32 [256, 256, 128], P('slab', 'col'), may hold values from 0 to 8191
- recv_index: int32 [32, 8, 32, 256], P('slab', 'col'), may hold values from 0 to 128
- coarse_diag: float32 [32, 8, 128, 128], P('slab', 'col'), as said below
- coarse_lower: float32 [32, 8, 128, 128], P('slab', 'col'), as said below
Outputs:
- solution: float32 [256, 256, 128], P('slab', 'col')
The draws below stay inside these ranges and needn't reach their ends.
Inputs may be any that keep to these rules, and one draw needn't show every extreme that they name: stencil_weights[13] is positive at every cell and exceeds the sum of the magnitudes of the other 26 coefficients of that cell. A slot's owner is floor(send_slot / 256) along slab, its position send_slot mod 256. `recv_index`: the value 128 marks a slot that feeds no coarse unknown. `coarse_diag`: every block is symmetric; with coarse_lower the coarse system is diagonally dominant by rows. `coarse_lower`: the blocks of the first owner along slab are zero.
All inputs are finite; a program needn't handle non-finite values.
Results may differ from the reference program's by a relative error of at most 0.0003.
Values sent between devices are 32-bit elements; how exact they have to be, the bound alone decides.
No kernel may reach another device: no remote copies, remote signals or barrier semaphores. Data moves between devices by JAX's collectives and lax.ppermute only.
A program may use at most 64 MiB of HBM per device.

```python
import math
import jax
import jax.numpy as jnp
from jax import lax

CX = 8
CY = 32
CZ = 128
NC = 128
CAP = 256
SMOOTH = 3
NX = 256
NY = 256
N_SLAB = 32
N_COL = 8


def draw_stencil_weights(key, part):
    key_scale, key_spread, key_center = jax.random.split(key, 3)
    cell_scale = jnp.exp(jax.random.uniform(key_scale, (NX, NY, CZ), jnp.float32, math.log(0.03), math.log(0.3)))
    lowest = 0.0
    spread = jax.random.uniform(key_spread, (27, NX, NY, CZ), jnp.float32, lowest, 1.0)
    center = jax.random.uniform(key_center, (NX, NY, CZ), jnp.float32, 27.5, 32.0)
    result = -spread * cell_scale
    return result.at[13].set(center * cell_scale)


def group_labels(key):
    return jax.random.randint(jax.random.fold_in(key, 5), (N_SLAB, N_COL, NC), 0, 4)


def coupling_levels(key, lowest):
    labels = group_labels(key)
    earlier_labels = jnp.roll(labels, 1, axis=0)
    same_group = labels[..., :, None] == earlier_labels[..., None, :]
    group_factor = jnp.where(same_group, 1.0, 1.0 / 64.0).astype(jnp.float32)
    sub_key = jax.random.fold_in(key, 11)
    drawn = jax.random.uniform(sub_key, (N_SLAB, N_COL, NC, NC), jnp.float32, lowest * 64.0, 64.0)
    levels = jnp.floor(drawn) / 64.0 * group_factor
    not_first = (jnp.arange(N_SLAB) > 0).astype(jnp.float32)[:, None, None, None]
    return levels * not_first


def draw_coarse_lower(key, part):
    lowest = 0.3
    return -8.0 / NC * coupling_levels(key, lowest)


def draw_coarse_diag(key, part):
    lowest = 0.3
    shift_low = 0.03
    shift_high = 0.09
    levels = coupling_levels(key, lowest)
    labels = group_labels(key)
    own_group = labels[..., :, None] == labels[..., None, :]
    own_factor = jnp.where(own_group, 1.0, 1.0 / 64.0).astype(jnp.float32)
    lower_rows = jnp.sum(levels, axis=3)
    column_sums = jnp.sum(levels, axis=2)
    upper_rows = jnp.concatenate([column_sums[1:], jnp.zeros_like(column_sums[:1])], axis=0)
    raw_draw = jax.random.uniform(jax.random.fold_in(key, 23), (N_SLAB, N_COL, NC, NC), jnp.float32, 0.0, 64.0)
    raw_levels = jnp.floor(raw_draw) / 64.0
    identity = jnp.eye(NC, dtype=jnp.float32)
    within = (raw_levels + jnp.swapaxes(raw_levels, 2, 3)) * (1.0 - identity) * own_factor
    within_rows = jnp.sum(within, axis=3)
    shift = jax.random.uniform(jax.random.fold_in(key, 37), (N_SLAB, N_COL, NC), jnp.float32, shift_low, shift_high)
    diagonal = 3.0 / NC * within_rows + 8.0 / NC * (lower_rows + upper_rows) + shift
    return -3.0 / NC * within + identity * diagonal[..., None]


def with_ends(values, rng, low, high):
    place = [jax.random.randint(jax.random.fold_in(rng, axis), (), 0, length) for axis, length in enumerate(values.shape)]
    longest = values.shape.index(max(values.shape))
    neighbour = place[:longest] + [(place[longest] + 1) % values.shape[longest]] + place[longest + 1:]
    return values.at[tuple(place)].set(low).at[tuple(neighbour)].set(high)


def level_of(own_key, shape, shards, least, high):
    gain, own = 1.0, jax.random.fold_in(own_key, 6)
    for dim, parts in shards:
        heights = jnp.exp(jax.random.uniform(jax.random.fold_in(own, dim), (parts,), jnp.float32, least / len(shards), high / len(shards)))
        gain = gain * jnp.repeat(heights, shape[dim] // parts).reshape([-1 if axis == dim else 1 for axis in range(len(shape))])
    return gain


def scatter_about(rng, extent, width, reach, pieces=(), kind=jnp.bfloat16):
    factor_of = level_of(rng, extent, pieces, -0.22, 0.18) if pieces else 1.0
    values = jax.random.normal(rng, extent, jnp.float32) * width * factor_of
    return jnp.minimum(jnp.maximum(values, -reach), reach).astype(kind)


def setup_inputs(seed: int = 0) -> dict:
    key_list = jax.random.split(jax.random.key(seed), 8)
    right_side = scatter_about(key_list[0], (NX, NY, CZ), 1.0, 6.0, ((0, 32), (1, 8)), jnp.float32)
    stencil_weights = draw_stencil_weights(jax.random.fold_in(key_list[7], 71), 0)
    cheb_steps = jnp.clip(jnp.exp(jax.random.uniform(key_list[2], (2 * SMOOTH,), jnp.float32, math.log(0.4), math.log(1.0))), 0.4, 1.0)
    send_slot = with_ends(jax.random.randint(key_list[3], (NX, NY, CZ), 0, N_SLAB * CAP), jax.random.fold_in(key_list[3], 1), 0, (N_SLAB * CAP) - 1).astype(jnp.int32)
    recv_index = with_ends(jax.random.randint(key_list[4], (N_SLAB, N_COL, N_SLAB, CAP), 0, NC + 1), jax.random.fold_in(key_list[4], 1), 0, NC).astype(jnp.int32)
    coarse_diag = draw_coarse_diag(jax.random.fold_in(key_list[7], 71), 0)
    coarse_lower = draw_coarse_lower(jax.random.fold_in(key_list[7], 71), 0)
    return dict(right_side=right_side, stencil_weights=stencil_weights, cheb_steps=cheb_steps, send_slot=send_slot, recv_index=recv_index, coarse_diag=coarse_diag, coarse_lower=coarse_lower)


PRECISE = lax.Precision.HIGHEST

def stencil(values, weights):
    padded = jnp.pad(values, 1)
    size_x, size_y, size_z = values.shape
    summed = jnp.zeros_like(values)
    for offset in range(27):
        shift_x = offset // 9
        shift_y = offset // 3 % 3
        shift_z = offset % 3
        summed = summed + weights[offset] * padded[shift_x:shift_x + size_x, shift_y:shift_y + size_y, shift_z:shift_z + size_z]
    return summed

def sweeps(solution, right_side, weights, factors):
    center = weights[13]
    for sweep_index in range(factors.shape[0]):
        residue = right_side - stencil(solution, weights)
        solution = solution + factors[sweep_index] * residue / center
    return solution

def chain_solve(diag_blocks, lower_blocks, rhs_blocks):
    block_order = diag_blocks.shape[-1]

    def forward(state_pair, inputs):
        prev_schur, prev_rhs = state_pair
        diag_block, lower_block, rhs_block = inputs
        solved_mat = jnp.linalg.solve(prev_schur, lower_block.T)
        solved_vec = jnp.linalg.solve(prev_schur, prev_rhs)
        schur_block = diag_block - jnp.dot(lower_block, solved_mat, precision=PRECISE)
        rhs_new = rhs_block - jnp.dot(lower_block, solved_vec, precision=PRECISE)
        return ((schur_block, rhs_new), (schur_block, rhs_new))
    start_state = (jnp.eye(block_order, dtype=jnp.float32), jnp.zeros((block_order,), jnp.float32))
    ignored, (schurs, rhs_all) = lax.scan(forward, start_state, (diag_blocks, lower_blocks, rhs_blocks))
    lower_next = jnp.concatenate([lower_blocks[1:], jnp.zeros_like(lower_blocks[:1])], axis=0)

    def backward(next_value, inputs):
        schur_block, rhs_block, lower_after = inputs
        result = jnp.linalg.solve(schur_block, rhs_block - jnp.dot(lower_after.T, next_value, precision=PRECISE))
        return (result, result)
    ignored, chain_values = lax.scan(backward, jnp.zeros((block_order,), jnp.float32), (schurs, rhs_all, lower_next), reverse=True)
    return chain_values

def reference(right_side, stencil_weights, cheb_steps, send_slot, recv_index, coarse_diag, coarse_lower):
    smooth = sweeps(jnp.zeros_like(right_side), right_side, stencil_weights, cheb_steps[:SMOOTH])
    residue = right_side - stencil(smooth, stencil_weights)
    source = (jnp.arange(NX, dtype=jnp.int32) // CX)[:, None, None]
    column = (jnp.arange(NY, dtype=jnp.int32) // CY)[None, :, None]
    owner_dev = send_slot // CAP
    within = send_slot % CAP
    target = recv_index[owner_dev, column, source, within]
    global_id = (column * N_SLAB + owner_dev) * (NC + 1) + target
    coarse_rhs = jax.ops.segment_sum(residue.reshape(-1), global_id.reshape(-1), num_segments=N_COL * N_SLAB * (NC + 1))
    coarse_rhs = coarse_rhs.reshape(N_COL, N_SLAB, NC + 1)[:, :, :NC]
    chains = []
    for group in range(N_COL):
        chains.append(chain_solve(coarse_diag[:, group], coarse_lower[:, group], coarse_rhs[group]))
    coarse_x = jnp.stack(chains, axis=0)
    padded_x = jnp.concatenate([coarse_x, jnp.zeros((N_COL, N_SLAB, 1), jnp.float32)], axis=2)
    corrected = smooth + padded_x.reshape(-1)[global_id]
    return sweeps(corrected, right_side, stencil_weights, cheb_steps[SMOOTH:])
```

```python
import functools

import jax
import jax.numpy as jnp
from jax import lax
from jax.experimental import pallas as pl
from jax.experimental.pallas import tpu as pltpu
from jax.sharding import PartitionSpec as P

F32 = jnp.float32
BF16 = jnp.bfloat16


def nn(a, b):
    return lax.dot_general(a, b, (((1,), (0,)), ((), ())), preferred_element_type=F32)

def nt(a, b):
    return lax.dot_general(a, b, (((1,), (1,)), ((), ())), preferred_element_type=F32)

def split(a):
    high = a.astype(BF16)
    return high, (a - high.astype(F32)).astype(BF16)

def one_hot(index_row, size):
    width = index_row.shape[1]
    return (lax.broadcasted_iota(jnp.int32, (size, width), 0) == index_row).astype(F32).astype(BF16)

def pair(block, first):
    return jnp.concatenate([block[first : first + 1], block[first + 1 : first + 2]], axis=1)

def gather_rows(table, height, parts, high, low):

    rows = []
    for first in range(0, 8, 2):
        picked = nn(table, one_hot(pair(low, first), 128))
        value = picked[:height]
        for part in range(1, parts):
            value = value + picked[part * height : (part + 1) * height]
        mask = lax.broadcasted_iota(jnp.int32, (height, 256), 0) == pair(high, first)
        row = jnp.sum(jnp.where(mask, value, 0.0), axis=0, keepdims=True)
        rows += [row[:, :128], row[:, 128:]]
    return jnp.concatenate(rows, axis=0)

def lookup_kernel(slot_ref, table_ref, out_ref):
    table = table_ref[...].astype(F32).astype(BF16)

    @pl.loop(0, slot_ref.shape[0] // 8)
    def _(block):
        where = pl.ds(pl.multiple_of(block * 8, 8), 8)
        slot = slot_ref[where]
        found = gather_rows(table, 64, 1, slot >> 7, slot & 127)
        out_ref[where] = found.astype(jnp.int32)

def lookup(slot, table):
    return pl.pallas_call(
        lookup_kernel,
        out_shape=jax.ShapeDtypeStruct(slot.shape, jnp.int32),
        compiler_params=pltpu.CompilerParams(vmem_limit_bytes=16 * 2**20),
    )(slot, table)

def scatter_kernel(slot_ref, unknown_ref, value_ref, out_ref):
    def step(block, total):
        where = pl.ds(pl.multiple_of(block * 8, 8), 8)
        owner = slot_ref[where] >> 8
        unknown = unknown_ref[where]
        value = value_ref[where]
        for first in range(0, 8, 2):
            mask = lax.broadcasted_iota(jnp.int32, (32, 256), 0) == pair(owner, first)
            spread = jnp.where(mask, pair(value, first), 0.0)
            high, low = split(spread)
            total = total + nt(jnp.concatenate([high, low], axis=0), one_hot(pair(unknown, first), 128))
        return total

    total = lax.fori_loop(0, slot_ref.shape[0] // 8, step, jnp.zeros((64, 128), F32))
    out_ref[...] = total[:32] + total[32:]

def scatter(slot, unknown, value):
    return pl.pallas_call(
        scatter_kernel,
        out_shape=jax.ShapeDtypeStruct((32, 128), F32),
        compiler_params=pltpu.CompilerParams(vmem_limit_bytes=16 * 2**20),
    )(slot, unknown, value)

def gather_kernel(slot_ref, unknown_ref, table_ref, base_ref, out_ref):
    high, low = split(table_ref[...])
    table = jnp.concatenate([high, low], axis=0)

    @pl.loop(0, slot_ref.shape[0] // 8)
    def _(block):
        where = pl.ds(pl.multiple_of(block * 8, 8), 8)
        out_ref[where] = base_ref[where] + gather_rows(table, 32, 2, slot_ref[where] >> 8, unknown_ref[where])

def gather(slot, unknown, table, base):
    return pl.pallas_call(
        gather_kernel,
        out_shape=jax.ShapeDtypeStruct(base.shape, F32),
        compiler_params=pltpu.CompilerParams(vmem_limit_bytes=16 * 2**20),
    )(slot, unknown, table, base)


def mm3(form, a, b):
    ah, al = split(a)
    bh, bl = split(b)
    return form(ah, bh) + (form(ah, bl) + form(al, bh))

def mm1(a, b):
    return nn(a.astype(BF16), b.astype(BF16))

def norm1(e):
    return jnp.max(jnp.sum(jnp.abs(e), axis=0, keepdims=True))

def invert(count, get_a, x_ref, r_ref):

    n = 128
    rows = lax.broadcasted_iota(jnp.int32, (n, n), 0)
    cols = lax.broadcasted_iota(jnp.int32, (n, n), 1)
    eye = (rows == cols).astype(F32)

    def recip_row(a):
        return 1.0 / jnp.sum(a * eye, axis=0, keepdims=True)

    rho = jnp.float32(0)
    for b in range(count):
        a = get_a(b)
        r = eye - a * recip_row(a)
        r_ref[b] = r
        x_ref[b] = eye + r
        rho = jnp.maximum(rho, norm1(r))

    def square_cond(state):
        bound, steps = state
        return jnp.logical_and(bound > 2e-3, steps < 20)

    def square(state):
        bound, steps = state
        for b in range(count):
            r = r_ref[b].astype(BF16)
            r2 = nn(r, r)
            y = x_ref[b]
            r_ref[b] = r2
            x_ref[b] = y + nn(y.astype(BF16), r2.astype(BF16))
        return bound * bound, steps + 1

    lax.while_loop(square_cond, square, (rho, jnp.int32(0)))

    def residual():
        worst = jnp.float32(0)
        for b in range(count):
            e = eye - mm3(nn, get_a(b), x_ref[b])
            r_ref[b] = e
            worst = jnp.maximum(worst, norm1(e))
        return worst

    def correct():
        for b in range(count):
            x = x_ref[b]
            x_ref[b] = x + mm3(nn, x, r_ref[b])

    for b in range(count):
        d = recip_row(get_a(b))
        dcol = jnp.sum(eye * d, axis=1, keepdims=True)
        x_ref[b] = x_ref[b] * dcol
    first = residual()

    def restart():
        for b in range(count):
            a = get_a(b)
            x_ref[b] = eye * recip_row(a)
        return residual()

    first = lax.cond(first < 0.5, lambda: first, restart)

    def newton_cond(state):
        worst, steps = state
        return jnp.logical_and(worst > 2e-3, steps < 60)

    def newton(state):
        correct()
        return residual(), state[1] + 1

    lax.while_loop(newton_cond, newton, (first, jnp.int32(0)))
    correct()

def invert_kernel(a_ref, x_ref, r_ref):
    invert(1, lambda b: a_ref[b], x_ref, r_ref)

def invert_one(a):
    return pl.pallas_call(
        invert_kernel,
        out_shape=jax.ShapeDtypeStruct((1, 128, 128), F32),
        scratch_shapes=[pltpu.VMEM((1, 128, 128), F32)],
        compiler_params=pltpu.CompilerParams(vmem_limit_bytes=16 * 2**20),
    )(a)

def factor_kernel(count, diag_ref, lower_ref, out_ref, d_ref, l_ref, x_ref, r_ref):
    stride = 1
    while stride < count:
        gone = list(range(stride, count, 2 * stride))
        src_d = diag_ref if stride == 1 else d_ref
        src_l = lower_ref if stride == 1 else l_ref
        if stride > 1:
            invert(len(gone), lambda b: src_d[gone[b]], x_ref, r_ref)
        for b, j in enumerate(gone):
            inverse = diag_ref[j] if stride == 1 else x_ref[b]
            out_ref[j, 0:128] = inverse
            out_ref[j, 128:256] = mm3(nn, src_l[j].T, inverse)
            if j + stride < count:
                out_ref[j, 256:384] = mm3(nn, src_l[j + stride], inverse)
            else:
                out_ref[j, 256:384] = jnp.zeros((128, 128), F32)
        for i in range(0, count, 2 * stride):
            high = i + stride
            value = src_d[i] - mm3(nn, out_ref[high, 128:256], src_l[high])
            if i > 0:
                low = i - stride
                qt = out_ref[low, 256:384]
                value = value - mm3(nt, qt, src_l[i])
                l_ref[i] = -mm3(nn, qt, src_l[low])
            d_ref[i] = value
        stride *= 2
    invert(1, lambda b: d_ref[0], x_ref, r_ref)
    out_ref[0, 0:128] = x_ref[0]
    out_ref[0, 128:384] = jnp.zeros((256, 128), F32)

def factor(diag, lower):

    count = diag.shape[0]
    return pl.pallas_call(
        functools.partial(factor_kernel, count),
        out_shape=jax.ShapeDtypeStruct((count, 384, 128), F32),
        scratch_shapes=[
            pltpu.VMEM((count, 128, 128), F32),
            pltpu.VMEM((count, 128, 128), F32),
            pltpu.VMEM((count // 4, 128, 128), F32),
            pltpu.VMEM((count // 4, 128, 128), F32),
        ],
        compiler_params=pltpu.CompilerParams(vmem_limit_bytes=48 * 2**20),
    )(diag, lower)

def solve_kernel(count, factor_ref, rhs_ref, out_ref, r_ref):
    def row3(form, row, mat):
        rh, rl = split(row)
        mh, ml = split(mat)
        return form(rh, mh) + (form(rl, mh) + form(rh, ml))
    r_ref[...] = rhs_ref[...]
    stride = 1
    while stride < count:
        for j in range(stride, count, 2 * stride):
            t = row3(nt, r_ref[pl.ds(j, 1)], factor_ref[j, 128:384])
            r_ref[pl.ds(j - stride, 1)] = r_ref[pl.ds(j - stride, 1)] - t[:, :128]
            if j + stride < count:
                r_ref[pl.ds(j + stride, 1)] = r_ref[pl.ds(j + stride, 1)] - t[:, 128:]
        stride *= 2
    out_ref[0:1] = row3(nn, r_ref[0:1], factor_ref[0, 0:128])
    while stride > 1:
        stride //= 2
        for j in range(stride, count, 2 * stride):
            x = row3(nn, r_ref[pl.ds(j, 1)], factor_ref[j, 0:128])
            x = x - row3(nn, out_ref[pl.ds(j - stride, 1)], factor_ref[j, 128:256])
            if j + stride < count:
                x = x - row3(nn, out_ref[pl.ds(j + stride, 1)], factor_ref[j, 256:384])
            out_ref[pl.ds(j, 1)] = x

def solve(factors, rhs):
    count = rhs.shape[0]
    return pl.pallas_call(
        functools.partial(solve_kernel, count),
        out_shape=jax.ShapeDtypeStruct((count, 128), F32),
        scratch_shapes=[pltpu.VMEM((count, 128), F32)],
        compiler_params=pltpu.CompilerParams(vmem_limit_bytes=32 * 2**20),
    )(factors, rhs)


SMOOTH = 3


def extended_2(block, sides, width):
    for axis, dim in sides:
        count = lax.axis_size(axis)
        forward = [(i, i + 1) for i in range(count - 1)]
        backward = [(target, source) for source, target in forward]
        low = lax.ppermute(
            lax.slice_in_dim(block, block.shape[dim] - width, None, axis=dim), axis, forward
        )
        high = lax.ppermute(lax.slice_in_dim(block, 0, width, axis=dim), axis, backward)
        block = jnp.concatenate([low, block, high], axis=dim)
    return block


def apply_stencil(values, weights):
    extended = extended_2(values, (("slab", 0), ("col", 1)), 1)
    padded = jnp.pad(extended, ((0, 0), (0, 0), (1, 1)))
    size_x, size_y, size_z = values.shape
    summed = jnp.zeros_like(values)
    for offset in range(27):
        shift_x = offset // 9
        shift_y = offset // 3 % 3
        shift_z = offset % 3
        summed = (
            summed
            + weights[offset]
            * padded[
                shift_x : shift_x + size_x, shift_y : shift_y + size_y, shift_z : shift_z + size_z
            ]
        )
    return summed


def sweeps(solution, right_side, weights, factors):
    center = weights[13]
    for sweep_index in range(factors.shape[0]):
        residue = right_side - apply_stencil(solution, weights)
        solution = solution + factors[sweep_index] * residue / center
    return solution


def shards(
    right_side, stencil_weights, cheb_steps, send_slot, recv_index, coarse_diag, coarse_lower
):
    slab_count = lax.axis_size("slab")
    me = lax.axis_index("slab")
    cells_shape = right_side.shape
    diag, lower = coarse_diag[0, 0], coarse_lower[0, 0]
    inverse = invert_one(diag[None])[0]
    mine = jnp.where(me % 2 == 1, inverse, diag)
    every = lax.all_gather(jnp.concatenate([mine, lower])[None], "slab", axis=0, tiled=True)

    table = lax.all_to_all(recv_index[0, 0], "slab", split_axis=0, concat_axis=0, tiled=True)
    slot = send_slot.reshape(-1, 128)
    unknown = lookup(slot, table.reshape(-1, 128))

    smooth = cheb_steps[0] * right_side / stencil_weights[13]
    smooth = sweeps(smooth, right_side, stencil_weights, cheb_steps[1:SMOOTH])
    residue = right_side - apply_stencil(smooth, stencil_weights)
    partial = scatter(slot, unknown, residue.reshape(-1, 128))
    arrived = lax.all_to_all(partial, "slab", split_axis=0, concat_axis=0, tiled=True)
    mine_rhs = jnp.sum(arrived, axis=0, keepdims=True)
    rhs = lax.all_to_all(
        jnp.broadcast_to(mine_rhs, arrived.shape), "slab", split_axis=0, concat_axis=0, tiled=True
    )

    factors = factor(every[:, :128], every[:, 128:])
    coarse_x = solve(factors, rhs)
    corrected = gather(slot, unknown, coarse_x, smooth.reshape(-1, 128)).reshape(cells_shape)
    return sweeps(corrected, right_side, stencil_weights, cheb_steps[SMOOTH:])


def solution(mesh):
    placed = (
        P("slab", "col", None),
        P(None, "slab", "col", None),
        P(),
        P("slab", "col", None),
        P("slab", "col", None, None),
        P("slab", "col", None, None),
        P("slab", "col", None, None),
    )
    return jax.shard_map(
        shards, mesh=mesh, in_specs=placed, out_specs=P("slab", "col", None), check_vma=False
    )
```

```python
import functools

import jax
import jax.numpy as jnp
from jax import lax
from jax.experimental import pallas as pl
from jax.experimental.pallas import tpu as pltpu
from jax.sharding import PartitionSpec as P

F32 = jnp.float32
BF16 = jnp.bfloat16
ROWS = 40


def nn(a, b):
    return lax.dot_general(a, b, (((1,), (0,)), ((), ())), preferred_element_type=F32)

def nt(a, b):
    return lax.dot_general(a, b, (((1,), (1,)), ((), ())), preferred_element_type=F32)

def split(a):
    high = a.astype(BF16)
    return high, (a - high.astype(F32)).astype(BF16)

def one_hot(index_row, size):
    width = index_row.shape[1]
    return (lax.broadcasted_iota(jnp.int32, (size, width), 0) == index_row).astype(F32).astype(BF16)

def pair(block, first):
    return jnp.concatenate([block[first : first + 1], block[first + 1 : first + 2]], axis=1)

def gather_rows(table, height, parts, high, low):
    rows = []
    for first in range(0, 8, 2):
        picked = nn(table, one_hot(pair(low, first), 128))
        value = picked[:height]
        for part in range(1, parts):
            value = value + picked[part * height : (part + 1) * height]
        mask = lax.broadcasted_iota(jnp.int32, (height, 256), 0) == pair(high, first)
        row = jnp.sum(jnp.where(mask, value, 0.0), axis=0, keepdims=True)
        rows += [row[:, :128], row[:, 128:]]
    return jnp.concatenate(rows, axis=0)

def lookup_kernel(slot_ref, table_ref, out_ref):
    table = table_ref[...].astype(BF16)

    @pl.loop(0, slot_ref.shape[0] // 8)
    def _(block):
        where = pl.ds(pl.multiple_of(block * 8, 8), 8)
        slot = slot_ref[where]
        found = gather_rows(table, 64, 1, slot >> 7, slot & 127)
        out_ref[where] = found.astype(jnp.int32)

def lookup(slot, table):
    return pl.pallas_call(
        lookup_kernel,
        out_shape=jax.ShapeDtypeStruct(slot.shape, jnp.int32),
        compiler_params=pltpu.CompilerParams(vmem_limit_bytes=16 * 2**20),
    )(slot, table)

def scatter_kernel(slot_ref, value_ref, out_ref):
    def step(block, total):
        where = pl.ds(pl.multiple_of(block * 8, 8), 8)
        slot = slot_ref[where]
        high_slot, low_slot = slot >> 7, slot & 127
        value = value_ref[where]
        for first in range(0, 8, 2):
            mask = lax.broadcasted_iota(jnp.int32, (64, 256), 0) == pair(high_slot, first)
            spread = jnp.where(mask, pair(value, first), 0.0)
            high, low = split(spread)
            total = total + nt(jnp.concatenate([high, low], axis=0), one_hot(pair(low_slot, first), 128))
        return total

    total = lax.fori_loop(0, slot_ref.shape[0] // 8, step, jnp.zeros((128, 128), F32))
    out_ref[...] = total[:64] + total[64:]


def scatter(slot, value):
    return pl.pallas_call(
        scatter_kernel,
        out_shape=jax.ShapeDtypeStruct((64, 128), F32),
        compiler_params=pltpu.CompilerParams(vmem_limit_bytes=16 * 2**20),
    )(slot, value)


def collect_kernel(index_ref, value_ref, out_ref):
    total = jnp.zeros((16, 128), F32)
    for first in range(0, 64, 2):
        row = pair(value_ref[...], first)
        high, low = split(jnp.concatenate([row] * 8, axis=0))
        spread = jnp.concatenate([high, low], axis=0)
        total = total + nt(spread, one_hot(pair(index_ref[...], first), 128))
    row = total[0:1] + total[8:9]
    out_ref[...] = jnp.concatenate([row] * 32, axis=0)


def collect(index, value):
    return pl.pallas_call(
        collect_kernel,
        out_shape=jax.ShapeDtypeStruct((32, 128), F32),
        compiler_params=pltpu.CompilerParams(vmem_limit_bytes=16 * 2**20),
    )(index, value)


def gather_kernel(slot_ref, unknown_ref, table_ref, base_ref, out_ref):
    high, low = split(table_ref[...])
    table = jnp.concatenate([high, low], axis=0)

    @pl.loop(0, slot_ref.shape[0] // 8)
    def _(block):
        where = pl.ds(pl.multiple_of(block * 8, 8), 8)
        out_ref[where] = base_ref[where] + gather_rows(table, 32, 2, slot_ref[where] >> 8, unknown_ref[where])

def gather(slot, unknown, table, base):
    return pl.pallas_call(
        gather_kernel,
        out_shape=jax.ShapeDtypeStruct(base.shape, F32),
        compiler_params=pltpu.CompilerParams(vmem_limit_bytes=16 * 2**20),
    )(slot, unknown, table, base)


def mm3(form, a, b):
    ah, al = split(a)
    bh, bl = split(b)
    return form(ah, bh) + (form(ah, bl) + form(al, bh))

def mm1(a, b):
    return nn(a.astype(BF16), b.astype(BF16))

def norm1(e):
    return jnp.max(jnp.sum(jnp.abs(e), axis=0, keepdims=True))

def invert(count, get_a, x_ref, r_ref):
    n = 128
    rows = lax.broadcasted_iota(jnp.int32, (n, n), 0)
    cols = lax.broadcasted_iota(jnp.int32, (n, n), 1)
    eye = (rows == cols).astype(F32)

    def recip_row(a):
        return 1.0 / jnp.sum(a * eye, axis=0, keepdims=True)

    rho = jnp.float32(0)
    for b in range(count):
        a = get_a(b)
        r = eye - a * recip_row(a)
        r_ref[b] = r
        x_ref[b] = eye + r
        rho = jnp.maximum(rho, norm1(r))

    def square_cond(state):
        bound, steps = state
        return jnp.logical_and(bound > 2e-3, steps < 20)

    def square(state):
        bound, steps = state
        for b in range(count):
            r = r_ref[b].astype(BF16)
            r2 = nn(r, r)
            y = x_ref[b]
            r_ref[b] = r2
            x_ref[b] = y + nn(y.astype(BF16), r2.astype(BF16))
        return bound * bound, steps + 1

    lax.while_loop(square_cond, square, (rho, jnp.int32(0)))

    def residual():
        worst = jnp.float32(0)
        for b in range(count):
            e = eye - mm3(nn, get_a(b), x_ref[b])
            r_ref[b] = e
            worst = jnp.maximum(worst, norm1(e))
        return worst

    def correct():
        for b in range(count):
            x = x_ref[b]
            x_ref[b] = x + mm3(nn, x, r_ref[b])

    for b in range(count):
        d = recip_row(get_a(b))
        dcol = jnp.sum(eye * d, axis=1, keepdims=True)
        x_ref[b] = x_ref[b] * dcol
    first = residual()

    def restart():
        for b in range(count):
            a = get_a(b)
            x_ref[b] = eye * recip_row(a)
        return residual()

    first = lax.cond(first < 0.5, lambda: first, restart)

    def newton_cond(state):
        worst, steps = state
        return jnp.logical_and(worst > 2e-3, steps < 60)

    def newton(state):
        correct()
        return residual(), state[1] + 1

    lax.while_loop(newton_cond, newton, (first, jnp.int32(0)))
    correct()

def invert_kernel(a_ref, x_ref, r_ref):
    invert(1, lambda b: a_ref[b], x_ref, r_ref)

def invert_one(a):
    return pl.pallas_call(
        invert_kernel,
        out_shape=jax.ShapeDtypeStruct((1, 128, 128), F32),
        scratch_shapes=[pltpu.VMEM((1, 128, 128), F32)],
        compiler_params=pltpu.CompilerParams(vmem_limit_bytes=16 * 2**20),
    )(a)

def factor_kernel(count, every_ref, out_ref, d_ref, l_ref, x_ref, r_ref):
    diag_ref = every_ref.at[:, 0:128]
    lower_ref = every_ref.at[:, 128:256]
    stride = 1
    while stride < count:
        gone = list(range(stride, count, 2 * stride))
        src_d = diag_ref if stride == 1 else d_ref
        src_l = lower_ref if stride == 1 else l_ref
        if stride > 1:
            invert(len(gone), lambda b: src_d[gone[b]], x_ref, r_ref)
        for b, j in enumerate(gone):
            inverse = diag_ref[j] if stride == 1 else x_ref[b]
            out_ref[j, 0:128] = inverse
            out_ref[j, 128:256] = mm3(nn, src_l[j].T, inverse)
            if j + stride < count:
                out_ref[j, 256:384] = mm3(nn, src_l[j + stride], inverse)
            else:
                out_ref[j, 256:384] = jnp.zeros((128, 128), F32)
        for i in range(0, count, 2 * stride):
            high = i + stride
            value = src_d[i] - mm3(nn, out_ref[high, 128:256], src_l[high])
            if i > 0:
                low = i - stride
                qt = out_ref[low, 256:384]
                value = value - mm3(nt, qt, src_l[i])
                l_ref[i] = -mm3(nn, qt, src_l[low])
            d_ref[i] = value
        stride *= 2
    invert(1, lambda b: d_ref[0], x_ref, r_ref)
    out_ref[0, 0:128] = x_ref[0]
    out_ref[0, 128:384] = jnp.zeros((256, 128), F32)

def factor(every):
    count = every.shape[0]
    return pl.pallas_call(
        functools.partial(factor_kernel, count),
        out_shape=jax.ShapeDtypeStruct((count, 384, 128), F32),
        scratch_shapes=[
            pltpu.VMEM((count, 128, 128), F32),
            pltpu.VMEM((count, 128, 128), F32),
            pltpu.VMEM((count // 4, 128, 128), F32),
            pltpu.VMEM((count // 4, 128, 128), F32),
        ],
        compiler_params=pltpu.CompilerParams(vmem_limit_bytes=48 * 2**20),
    )(every)

def solve_kernel(count, factor_ref, rhs_ref, out_ref, r_ref):
    def row3(form, row, mat):
        rh, rl = split(row)
        mh, ml = split(mat)
        return form(rh, mh) + (form(rl, mh) + form(rh, ml))
    r_ref[...] = rhs_ref[...]
    stride = 1
    while stride < count:
        for j in range(stride, count, 2 * stride):
            t = row3(nt, r_ref[pl.ds(j, 1)], factor_ref[j, 128:384])
            r_ref[pl.ds(j - stride, 1)] = r_ref[pl.ds(j - stride, 1)] - t[:, :128]
            if j + stride < count:
                r_ref[pl.ds(j + stride, 1)] = r_ref[pl.ds(j + stride, 1)] - t[:, 128:]
        stride *= 2
    out_ref[0:1] = row3(nn, r_ref[0:1], factor_ref[0, 0:128])
    while stride > 1:
        stride //= 2
        for j in range(stride, count, 2 * stride):
            x = row3(nn, r_ref[pl.ds(j, 1)], factor_ref[j, 0:128])
            x = x - row3(nn, out_ref[pl.ds(j - stride, 1)], factor_ref[j, 128:256])
            if j + stride < count:
                x = x - row3(nn, out_ref[pl.ds(j + stride, 1)], factor_ref[j, 256:384])
            out_ref[pl.ds(j, 1)] = x

def solve(factors, rhs):
    count = rhs.shape[0]
    return pl.pallas_call(
        functools.partial(solve_kernel, count),
        out_shape=jax.ShapeDtypeStruct((count, 128), F32),
        scratch_shapes=[pltpu.VMEM((count, 128), F32)],
        compiler_params=pltpu.CompilerParams(vmem_limit_bytes=32 * 2**20),
    )(factors, rhs)


def cut_kernel(weights_ref, side_ref, next_ref, previous_ref, start_ref):
    for offset in range(27):
        for x in range(8):
            next_ref[8 * offset + x] = weights_ref[offset, x, 30:32]
            previous_ref[8 * offset + x] = weights_ref[offset, x, 0:2]
    for x in range(8):
        start_ref[x] = side_ref[x] / weights_ref[13, x]
        next_ref[216 + x] = side_ref[x, 30:32]
        previous_ref[216 + x] = side_ref[x, 0:2]
        next_ref[224 + x] = start_ref[x, 29:31]
        next_ref[232 + x] = start_ref[x, 30:32]
        previous_ref[224 + x] = start_ref[x, 0:2]
        previous_ref[232 + x] = start_ref[x, 1:3]


def cut(weights, side):
    rows = jax.ShapeDtypeStruct((240, 2, 128), F32)
    return pl.pallas_call(
        cut_kernel,
        out_shape=(rows, rows, jax.ShapeDtypeStruct((8, 32, 128), F32)),
        compiler_params=pltpu.CompilerParams(vmem_limit_bytes=32 * 2**20),
    )(weights, side)


def pack_kernel(
    weights_ref, side_ref, start_ref, left_ref, right_ref,
    next_ref, previous_ref, edge_ref, edge_start_ref,
):
    edge_ref[...] = jnp.zeros((224, 8, 128), F32)
    edge_start_ref[...] = jnp.zeros((8, 8, 128), F32)

    @pl.loop(0, 224)
    def _(k):
        edge_ref[k, 0:2] = right_ref[k]
        edge_ref[k, 6:8] = left_ref[k]

    for x in range(8):
        edge_start_ref[x, 0:2] = right_ref[224 + x]
        edge_start_ref[x, 1:3] = right_ref[232 + x]
        edge_start_ref[x, 5:7] = left_ref[224 + x]
        edge_start_ref[x, 6:8] = left_ref[232 + x]

    @pl.loop(0, 27)
    def _(offset):
        for x in range(2):
            next_ref[2 * offset + x, :32] = weights_ref[offset, 6 + x]
            next_ref[2 * offset + x, 32:] = edge_ref[8 * offset + 6 + x]
            previous_ref[2 * offset + x, :32] = weights_ref[offset, x]
            previous_ref[2 * offset + x, 32:] = edge_ref[8 * offset + x]

    for x in range(2):
        next_ref[54 + x, :32] = side_ref[6 + x]
        next_ref[54 + x, 32:] = edge_ref[222 + x]
        previous_ref[54 + x, :32] = side_ref[x]
        previous_ref[54 + x, 32:] = edge_ref[216 + x]
    for x in range(3):
        next_ref[56 + x, :32] = start_ref[5 + x]
        next_ref[56 + x, 32:] = edge_start_ref[5 + x]
        previous_ref[56 + x, :32] = start_ref[x]
        previous_ref[56 + x, 32:] = edge_start_ref[x]


def pack(weights, side, start, left, right):
    planes = jax.ShapeDtypeStruct((59, ROWS, 128), F32)
    return pl.pallas_call(
        pack_kernel,
        out_shape=(
            planes, planes,
            jax.ShapeDtypeStruct((224, 8, 128), F32), jax.ShapeDtypeStruct((8, 8, 128), F32),
        ),
        compiler_params=pltpu.CompilerParams(vmem_limit_bytes=40 * 2**20),
    )(weights, side, start, left, right)


def shifted_planes(values_ref, shifted_ref, first, count):
    lane = lax.broadcasted_iota(jnp.int32, (ROWS, 128), 1)

    @pl.loop(first, first + count)
    def _(x):
        plane = values_ref[x]
        below = jnp.where(lane == 0, 0.0, pltpu.roll(plane, 1, 1))
        above = jnp.where(lane == 127, 0.0, pltpu.roll(plane, 127, 1))
        for c, along_z in enumerate((below, plane, above)):
            shifted_ref[c, x] = pltpu.roll(along_z, 1, 0)
            shifted_ref[3 + c, x] = along_z
            shifted_ref[6 + c, x] = pltpu.roll(along_z, ROWS - 1, 0)


def product(weight, shifted_ref, x, begin, end):
    total = None
    for a in range(3):
        for k in range(9):
            term = weight(9 * a + k) * shifted_ref[k, x + a, begin:end]
            total = term if total is None else total + term
    return total


def sweep(halo, side_ref, inverse_ref, values_ref, shifted_ref, factor, reach):
    main_ref, edge_ref, low_ref, high_ref = halo
    shifted_planes(values_ref, shifted_ref, 2 - reach, 10 + 2 * reach)

    def update(weight, x, begin, end):
        rest = side_ref[x, begin:end] - product(weight, shifted_ref, x, begin, end)
        old = values_ref[x + 1, begin:end]
        values_ref[x + 1, begin:end] = old + factor * rest * inverse_ref[x, begin:end]

    for x in range(2 - reach, 2):
        update(lambda o: low_ref[2 * o + x], x, 0, ROWS)
    for x in range(10, 10 + reach):
        update(lambda o: high_ref[2 * o + x - 10], x, 0, ROWS)

    @pl.loop(0, 8)
    def _(x):
        update(lambda o: main_ref[o, x], x + 2, 0, 32)
        if reach:
            update(lambda o: edge_ref[8 * o + x], x + 2, 32, ROWS)


def pre_kernel(
    steps_ref, main_ref, edge_ref, low_ref, high_ref, side_main_ref, start_ref, edge_start_ref,
    smooth_ref, residue_ref, side_ref, inverse_ref, values_ref, shifted_ref,
):
    def inverse(center):
        return jnp.where(center > 0, 1.0 / jnp.where(center > 0, center, 1.0), 0.0)

    scale = steps_ref[0]
    for x in range(2):
        side_ref[x] = low_ref[54 + x]
        side_ref[10 + x] = high_ref[54 + x]
        inverse_ref[x] = inverse(low_ref[26 + x])
        inverse_ref[10 + x] = inverse(high_ref[26 + x])
    for x in range(8):
        side_ref[2 + x, :32] = side_main_ref[x]
        side_ref[2 + x, 32:] = edge_ref[216 + x]
        inverse_ref[2 + x, :32] = inverse(main_ref[13, x])
        inverse_ref[2 + x, 32:] = inverse(edge_ref[104 + x])
        values_ref[3 + x, :32] = scale * start_ref[x]
        values_ref[3 + x, 32:] = scale * edge_start_ref[x]
    for x in range(3):
        values_ref[x] = scale * low_ref[56 + x]
        values_ref[11 + x] = scale * high_ref[56 + x]
    halo = main_ref, edge_ref, low_ref, high_ref
    sweep(halo, side_ref, inverse_ref, values_ref, shifted_ref, steps_ref[1], 2)
    sweep(halo, side_ref, inverse_ref, values_ref, shifted_ref, steps_ref[2], 1)
    shifted_planes(values_ref, shifted_ref, 2, 10)

    @pl.loop(0, 8)
    def _(x):
        smooth_ref[x] = values_ref[x + 3, :32]
        residue_ref[x] = side_main_ref[x] - product(lambda o: main_ref[o, x], shifted_ref, x + 2, 0, 32)


def stencil_scratch():
    return [pltpu.VMEM((14, ROWS, 128), F32), pltpu.VMEM((9, 14, ROWS, 128), F32)]


def pre_smooth(steps, weights, edge, low, high, side, start, edge_start):
    cells = jax.ShapeDtypeStruct((8, 32, 128), F32)
    outside = jax.ShapeDtypeStruct((12, ROWS, 128), F32)
    vmem = pl.BlockSpec(memory_space=pltpu.VMEM)
    return pl.pallas_call(
        pre_kernel,
        out_shape=(cells, cells, outside, outside),
        in_specs=[pl.BlockSpec(memory_space=pltpu.SMEM)] + [vmem] * 7,
        scratch_shapes=stencil_scratch(),
        compiler_params=pltpu.CompilerParams(vmem_limit_bytes=40 * 2**20),
    )(steps, weights, edge, low, high, side, start, edge_start)


def post_kernel(
    steps_ref, main_ref, edge_ref, low_ref, high_ref, side_ref, inverse_ref,
    cells_ref, below_ref, beyond_ref, left_ref, right_ref,
    out_ref, values_ref, shifted_ref,
):
    values_ref[:, 32:40] = jnp.zeros((14, 8, 128), F32)
    for x in range(3):
        values_ref[x, :32] = below_ref[x]
        values_ref[11 + x, :32] = beyond_ref[x]
    for x in range(8):
        values_ref[3 + x, :32] = cells_ref[x]
    for x in range(14):
        values_ref[x, 32:35] = right_ref[x]
        values_ref[x, 37:40] = left_ref[x]
    halo = main_ref, edge_ref, low_ref, high_ref
    sweep(halo, side_ref, inverse_ref, values_ref, shifted_ref, steps_ref[3], 2)
    sweep(halo, side_ref, inverse_ref, values_ref, shifted_ref, steps_ref[4], 1)
    sweep(halo, side_ref, inverse_ref, values_ref, shifted_ref, steps_ref[5], 0)
    out_ref[...] = values_ref[3:11, :32]


def post_smooth(steps, weights, edge, low, high, side, inverse, cells, below, beyond, left, right):
    vmem = pl.BlockSpec(memory_space=pltpu.VMEM)
    return pl.pallas_call(
        post_kernel,
        out_shape=jax.ShapeDtypeStruct((8, 32, 128), F32),
        in_specs=[pl.BlockSpec(memory_space=pltpu.SMEM)] + [vmem] * 11,
        scratch_shapes=stencil_scratch(),
        compiler_params=pltpu.CompilerParams(vmem_limit_bytes=40 * 2**20),
    )(steps, weights, edge, low, high, side, inverse, cells, below, beyond, left, right)


SMOOTH = 3


def from_sides(axis, to_next, to_previous):
    count = lax.axis_size(axis)
    forward = [(i, i + 1) for i in range(count - 1)]
    backward = [(target, source) for source, target in forward]
    return lax.ppermute(to_next, axis, forward), lax.ppermute(to_previous, axis, backward)


def halo_values(values):
    low, high = from_sides("slab", values[5:], values[:3])

    def rows(first):
        return jnp.concatenate(
            [low[:, first : first + 3], values[:, first : first + 3], high[:, first : first + 3]],
            axis=0,
        )

    left, right = from_sides("col", rows(29), rows(0))
    return low, high, left, right


def shards(
    right_side, stencil_weights, cheb_steps, send_slot, recv_index, coarse_diag, coarse_lower
):
    me = lax.axis_index("slab")
    diag, lower = coarse_diag[0, 0], coarse_lower[0, 0]
    index = recv_index.reshape(64, 128)
    inverse = invert_one(diag[None])[0]
    mine = jnp.where(me % 2 == 1, inverse, diag)
    blocks = jnp.concatenate([mine, lower, index.astype(F32)])
    every = lax.all_gather(blocks[None], "slab", axis=0, tiled=True)

    to_next, to_previous, start = cut(stencil_weights, right_side)
    left, right = from_sides("col", to_next, to_previous)
    to_next, to_previous, edge, edge_start = pack(stencil_weights, right_side, start, left, right)
    low, high = from_sides("slab", to_next, to_previous)
    smooth, residue, side, inverse_center = pre_smooth(
        cheb_steps, stencil_weights, edge, low, high, right_side, start, edge_start
    )
    slot = send_slot.reshape(-1, 128)
    sums = scatter(slot, residue.reshape(-1, 128)).reshape(32, 256)
    arrived = lax.all_to_all(sums, "slab", split_axis=0, concat_axis=0, tiled=True)
    mine_rhs = collect(index, arrived.reshape(64, 128))
    rhs = lax.all_to_all(mine_rhs, "slab", split_axis=0, concat_axis=0, tiled=True)

    table = lax.dynamic_slice_in_dim(every, 256 + 2 * me, 2, axis=1).reshape(64, 128)
    unknown = lookup(slot, table)
    coarse_x = solve(factor(every), rhs)
    corrected = gather(slot, unknown, coarse_x, smooth.reshape(-1, 128)).reshape(right_side.shape)
    return post_smooth(
        cheb_steps, stencil_weights, edge, low, high, side, inverse_center,
        corrected, *halo_values(corrected),
    )


def solution(mesh):
    placed = (
        P("slab", "col", None),
        P(None, "slab", "col", None),
        P(),
        P("slab", "col", None),
        P("slab", "col", None, None),
        P("slab", "col", None, None),
        P("slab", "col", None, None),
    )
    return jax.shard_map(
        shards, mesh=mesh, in_specs=placed, out_specs=P("slab", "col", None), check_vma=False
    )
```

```python
import functools

import jax
import jax.numpy as jnp
from jax import lax
from jax.experimental import pallas as pl
from jax.experimental.pallas import tpu as pltpu
from jax.sharding import PartitionSpec as P

F32 = jnp.float32
BF16 = jnp.bfloat16
ROWS = 40
SMOOTH = 3


def nn(a, b):
    return lax.dot_general(a, b, (((1,), (0,)), ((), ())), preferred_element_type=F32)

def nt(a, b):
    return lax.dot_general(a, b, (((1,), (1,)), ((), ())), preferred_element_type=F32)

def split(a):
    high = a.astype(BF16)
    return high, (a - high.astype(F32)).astype(BF16)

def one_hot(index_row, size):
    width = index_row.shape[1]
    wide = jnp.broadcast_to(index_row.astype(F32), (size, width)).astype(BF16)
    rows = lax.broadcasted_iota(jnp.int32, (size, width), 0).astype(F32).astype(BF16)
    return jnp.where(rows == wide, jnp.bfloat16(1), jnp.bfloat16(0))

def pair(block, first):
    return jnp.concatenate([block[first : first + 1], block[first + 1 : first + 2]], axis=1)

def gather_rows(table, height, parts, high, low):
    rows = []
    for first in range(0, 8, 2):
        picked = nn(table, one_hot(pair(low, first), 128))
        value = picked[:height]
        for part in range(1, parts):
            value = value + picked[part * height : (part + 1) * height]
        mask = lax.broadcasted_iota(jnp.int32, (height, 256), 0) == pair(high, first)
        row = jnp.sum(jnp.where(mask, value, 0.0), axis=0, keepdims=True)
        rows += [row[:, :128], row[:, 128:]]
    return jnp.concatenate(rows, axis=0)

def slot_row(slot):
    return ((slot >> 7) & 1) * 32 + (slot >> 8)


def lookup_kernel(slot_ref, table_ref, out_ref):
    table = table_ref[...].astype(BF16)

    @pl.loop(0, slot_ref.shape[0] // 8, unroll=8)
    def _(block):
        where = pl.ds(pl.multiple_of(block * 8, 8), 8)
        slot = slot_ref[where]
        found = gather_rows(table, 64, 1, slot_row(slot), slot & 127)
        out_ref[where] = found.astype(jnp.int32)


def lookup(slot, table):
    return pl.pallas_call(
        lookup_kernel,
        out_shape=jax.ShapeDtypeStruct(slot.shape, jnp.int32),
        compiler_params=pltpu.CompilerParams(vmem_limit_bytes=8 * 2**20),
    )(slot, table)


def scatter_kernel(slot_ref, value_ref, out_ref):
    def step(block, total):
        where = pl.ds(pl.multiple_of(block * 8, 8), 8)
        slot = slot_ref[where]
        high_slot, low_slot = slot_row(slot), slot & 127
        value = value_ref[where]
        value_high = value.astype(BF16).astype(F32)
        value_low = value - value_high
        for first in range(0, 8, 2):
            mask = lax.broadcasted_iota(jnp.int32, (64, 256), 0) == pair(high_slot, first)
            high = jnp.where(mask, pair(value_high, first), 0.0).astype(BF16)
            low = jnp.where(mask, pair(value_low, first), 0.0).astype(BF16)
            total = total + nt(jnp.concatenate([high, low], axis=0), one_hot(pair(low_slot, first), 128))
        return total

    total = lax.fori_loop(0, slot_ref.shape[0] // 8, step, jnp.zeros((128, 128), F32), unroll=8)
    total = total[:64] + total[64:]
    out_ref[...] = jnp.concatenate([total[:32], total[32:]], axis=1)


def scatter(slot, value):
    return pl.pallas_call(
        scatter_kernel,
        out_shape=jax.ShapeDtypeStruct((32, 256), F32),
        compiler_params=pltpu.CompilerParams(vmem_limit_bytes=8 * 2**20),
    )(slot, value)


def collect_kernel(index_ref, value_ref, out_ref):
    total = jnp.zeros((16, 128), F32)
    for source in range(32):
        row = value_ref[source : source + 1]
        high, low = split(jnp.concatenate([row] * 8, axis=0))
        spread = jnp.concatenate([high, low], axis=0)
        total = total + nt(spread, one_hot(index_ref[source : source + 1], 128))
    row = total[0:1] + total[8:9]
    out_ref[...] = jnp.concatenate([row] * 32, axis=0)


def collect(index, value):
    return pl.pallas_call(
        collect_kernel,
        out_shape=jax.ShapeDtypeStruct((32, 128), F32),
        compiler_params=pltpu.CompilerParams(vmem_limit_bytes=8 * 2**20),
    )(index, value)


def gather_kernel(slot_ref, unknown_ref, table_ref, base_ref, out_ref):
    high, low = split(table_ref[...])
    table = jnp.concatenate([high, low], axis=0)

    @pl.loop(0, slot_ref.shape[0] // 8, unroll=8)
    def _(block):
        where = pl.ds(pl.multiple_of(block * 8, 8), 8)
        rows = pl.ds(pl.multiple_of((block % 4) * 8, 8), 8)
        found = gather_rows(table, 32, 2, slot_ref[where] >> 8, unknown_ref[where])
        out_ref[block // 4, rows] = base_ref[block // 4, rows] + found


def gather(slot, unknown, table, base):
    return pl.pallas_call(
        gather_kernel,
        out_shape=jax.ShapeDtypeStruct(base.shape, F32),
        compiler_params=pltpu.CompilerParams(vmem_limit_bytes=8 * 2**20),
    )(slot, unknown, table, base)


def mm3(form, a, b):
    ah, al = split(a)
    bh, bl = split(b)
    return form(ah, bh) + (form(ah, bl) + form(al, bh))

def mm1(a, b):
    return nn(a.astype(BF16), b.astype(BF16))

def norm1(e):
    return jnp.max(jnp.sum(jnp.abs(e), axis=0, keepdims=True))

def invert(count, get_a, x_ref, r_ref):
    n = 128
    rows = lax.broadcasted_iota(jnp.int32, (n, n), 0)
    cols = lax.broadcasted_iota(jnp.int32, (n, n), 1)
    eye = (rows == cols).astype(F32)

    def recip_row(a):
        return 1.0 / jnp.sum(a * eye, axis=0, keepdims=True)

    rho = jnp.float32(0)
    for b in range(count):
        a = get_a(b)
        r = eye - a * recip_row(a)
        r_ref[b] = r
        x_ref[b] = eye + r
        rho = jnp.maximum(rho, norm1(r))

    def square_cond(state):
        bound, steps = state
        return jnp.logical_and(bound > 2e-3, steps < 20)

    def square(state):
        bound, steps = state
        for b in range(count):
            r = r_ref[b].astype(BF16)
            r2 = nn(r, r)
            y = x_ref[b]
            r_ref[b] = r2
            x_ref[b] = y + nn(y.astype(BF16), r2.astype(BF16))
        return bound * bound, steps + 1

    lax.while_loop(square_cond, square, (rho, jnp.int32(0)))

    def residual():
        worst = jnp.float32(0)
        for b in range(count):
            e = eye - mm3(nn, get_a(b), x_ref[b])
            r_ref[b] = e
            worst = jnp.maximum(worst, norm1(e))
        return worst

    def correct():
        for b in range(count):
            x = x_ref[b]
            x_ref[b] = x + mm3(nn, x, r_ref[b])

    for b in range(count):
        d = recip_row(get_a(b))
        dcol = jnp.sum(eye * d, axis=1, keepdims=True)
        x_ref[b] = x_ref[b] * dcol
    first = residual()

    def restart():
        for b in range(count):
            a = get_a(b)
            x_ref[b] = eye * recip_row(a)
        return residual()

    first = lax.cond(first < 0.5, lambda: first, restart)

    def newton_cond(state):
        worst, steps = state
        return jnp.logical_and(worst > 2e-3, steps < 60)

    def newton(state):
        correct()
        return residual(), state[1] + 1

    lax.while_loop(newton_cond, newton, (first, jnp.int32(0)))
    correct()

def blocks_kernel(place_ref, diag_ref, lower_ref, index_ref, out_ref, x_ref, r_ref):
    invert(1, lambda b: diag_ref[...], x_ref, r_ref)
    odd = place_ref[0] % 2 == 1
    out_ref[0:128] = jnp.where(odd, x_ref[0], diag_ref[...])
    out_ref[128:256] = lower_ref[...]
    out_ref[256:288] = index_ref[:, :128].astype(F32)
    out_ref[288:320] = index_ref[:, 128:].astype(F32)


def own_blocks(place, diag, lower, index):
    vmem = pl.BlockSpec(memory_space=pltpu.VMEM)
    return pl.pallas_call(
        blocks_kernel,
        out_shape=jax.ShapeDtypeStruct((320, 128), F32),
        in_specs=[pl.BlockSpec(memory_space=pltpu.SMEM), vmem, vmem, vmem],
        scratch_shapes=[pltpu.VMEM((1, 128, 128), F32), pltpu.VMEM((1, 128, 128), F32)],
        compiler_params=pltpu.CompilerParams(vmem_limit_bytes=4 * 2**20),
    )(place, diag, lower, index)


def factor_kernel(count, every_ref, out_ref, d_ref, l_ref, x_ref, r_ref):
    diag_ref = every_ref.at[:, 0:128]
    lower_ref = every_ref.at[:, 128:256]
    stride = 1
    while stride < count:
        gone = list(range(stride, count, 2 * stride))
        src_d = diag_ref if stride == 1 else d_ref
        src_l = lower_ref if stride == 1 else l_ref
        if stride > 1:
            invert(len(gone), lambda b: src_d[gone[b]], x_ref, r_ref)
        for b, j in enumerate(gone):
            inverse = diag_ref[j] if stride == 1 else x_ref[b]
            out_ref[j, 0:128] = inverse
            out_ref[j, 128:256] = mm3(nn, src_l[j].T, inverse)
            if j + stride < count:
                out_ref[j, 256:384] = mm3(nn, src_l[j + stride], inverse)
            else:
                out_ref[j, 256:384] = jnp.zeros((128, 128), F32)
        for i in range(0, count, 2 * stride):
            high = i + stride
            value = src_d[i] - mm3(nn, out_ref[high, 128:256], src_l[high])
            if i > 0:
                low = i - stride
                qt = out_ref[low, 256:384]
                value = value - mm3(nt, qt, src_l[i])
                l_ref[i] = -mm3(nn, qt, src_l[low])
            d_ref[i] = value
        stride *= 2
    invert(1, lambda b: d_ref[0], x_ref, r_ref)
    out_ref[0, 0:128] = x_ref[0]
    out_ref[0, 128:384] = jnp.zeros((256, 128), F32)

def factor(every):
    count = every.shape[0]
    return pl.pallas_call(
        functools.partial(factor_kernel, count),
        out_shape=jax.ShapeDtypeStruct((count, 384, 128), F32),
        scratch_shapes=[
            pltpu.VMEM((count, 128, 128), F32),
            pltpu.VMEM((count, 128, 128), F32),
            pltpu.VMEM((count // 4, 128, 128), F32),
            pltpu.VMEM((count // 4, 128, 128), F32),
        ],
        compiler_params=pltpu.CompilerParams(vmem_limit_bytes=22 * 2**20),
    )(every)


def solve_kernel(count, factor_ref, rhs_ref, out_ref, r_ref):
    def row3(form, row, mat):
        rh, rl = split(row)
        mh, ml = split(mat)
        return form(rh, mh) + (form(rl, mh) + form(rh, ml))
    r_ref[...] = rhs_ref[...]
    stride = 1
    while stride < count:
        for j in range(stride, count, 2 * stride):
            t = row3(nt, r_ref[pl.ds(j, 1)], factor_ref[j, 128:384])
            r_ref[pl.ds(j - stride, 1)] = r_ref[pl.ds(j - stride, 1)] - t[:, :128]
            if j + stride < count:
                r_ref[pl.ds(j + stride, 1)] = r_ref[pl.ds(j + stride, 1)] - t[:, 128:]
        stride *= 2
    out_ref[0:1] = row3(nn, r_ref[0:1], factor_ref[0, 0:128])
    while stride > 1:
        stride //= 2
        for j in range(stride, count, 2 * stride):
            x = row3(nn, r_ref[pl.ds(j, 1)], factor_ref[j, 0:128])
            x = x - row3(nn, out_ref[pl.ds(j - stride, 1)], factor_ref[j, 128:256])
            if j + stride < count:
                x = x - row3(nn, out_ref[pl.ds(j + stride, 1)], factor_ref[j, 256:384])
            out_ref[pl.ds(j, 1)] = x

def solve(factors, rhs):
    count = rhs.shape[0]
    return pl.pallas_call(
        functools.partial(solve_kernel, count),
        out_shape=jax.ShapeDtypeStruct((count, 128), F32),
        scratch_shapes=[pltpu.VMEM((count, 128), F32)],
        compiler_params=pltpu.CompilerParams(vmem_limit_bytes=10 * 2**20),
    )(factors, rhs)


def cut_kernel(weights_ref, side_ref, next_ref, previous_ref, start_ref):
    for offset in range(27):
        for x in range(8):
            next_ref[8 * offset + x] = weights_ref[offset, x, 30:32]
            previous_ref[8 * offset + x] = weights_ref[offset, x, 0:2]
    for x in range(8):
        start_ref[x] = side_ref[x] / weights_ref[13, x]
        next_ref[216 + x] = side_ref[x, 30:32]
        previous_ref[216 + x] = side_ref[x, 0:2]
        next_ref[224 + x] = start_ref[x, 29:31]
        next_ref[232 + x] = start_ref[x, 30:32]
        previous_ref[224 + x] = start_ref[x, 0:2]
        previous_ref[232 + x] = start_ref[x, 1:3]


def cut(weights, side):
    rows = jax.ShapeDtypeStruct((240, 2, 128), F32)
    return pl.pallas_call(
        cut_kernel,
        out_shape=(rows, rows, jax.ShapeDtypeStruct((8, 32, 128), F32)),
        compiler_params=pltpu.CompilerParams(vmem_limit_bytes=10 * 2**20),
    )(weights, side)


def pack_kernel(
    weights_ref, side_ref, start_ref, left_ref, right_ref,
    next_ref, previous_ref, edge_ref, edge_start_ref,
):
    edge_ref[...] = jnp.zeros((224, 8, 128), F32)
    edge_start_ref[...] = jnp.zeros((8, 8, 128), F32)

    @pl.loop(0, 224)
    def _(k):
        edge_ref[k, 0:2] = right_ref[k]
        edge_ref[k, 6:8] = left_ref[k]

    for x in range(8):
        edge_start_ref[x, 0:2] = right_ref[224 + x]
        edge_start_ref[x, 1:3] = right_ref[232 + x]
        edge_start_ref[x, 5:7] = left_ref[224 + x]
        edge_start_ref[x, 6:8] = left_ref[232 + x]

    @pl.loop(0, 27)
    def _(offset):
        for x in range(2):
            next_ref[2 * offset + x, :32] = weights_ref[offset, 6 + x]
            next_ref[2 * offset + x, 32:] = edge_ref[8 * offset + 6 + x]
            previous_ref[2 * offset + x, :32] = weights_ref[offset, x]
            previous_ref[2 * offset + x, 32:] = edge_ref[8 * offset + x]

    for x in range(2):
        next_ref[54 + x, :32] = side_ref[6 + x]
        next_ref[54 + x, 32:] = edge_ref[222 + x]
        previous_ref[54 + x, :32] = side_ref[x]
        previous_ref[54 + x, 32:] = edge_ref[216 + x]
    for x in range(3):
        next_ref[56 + x, :32] = start_ref[5 + x]
        next_ref[56 + x, 32:] = edge_start_ref[5 + x]
        previous_ref[56 + x, :32] = start_ref[x]
        previous_ref[56 + x, 32:] = edge_start_ref[x]


def pack(weights, side, start, left, right):
    planes = jax.ShapeDtypeStruct((59, ROWS, 128), F32)
    return pl.pallas_call(
        pack_kernel,
        out_shape=(
            planes, planes,
            jax.ShapeDtypeStruct((224, 8, 128), F32), jax.ShapeDtypeStruct((8, 8, 128), F32),
        ),
        compiler_params=pltpu.CompilerParams(vmem_limit_bytes=16 * 2**20),
    )(weights, side, start, left, right)


def shifted_planes(values_ref, shifted_ref, first, count):
    lane = lax.broadcasted_iota(jnp.int32, (ROWS, 128), 1)

    @pl.loop(first, first + count, unroll=2)
    def _(x):
        plane = values_ref[x]
        below = jnp.where(lane == 0, 0.0, pltpu.roll(plane, 1, 1))
        above = jnp.where(lane == 127, 0.0, pltpu.roll(plane, 127, 1))
        for c, along_z in enumerate((below, plane, above)):
            shifted_ref[c, x] = pltpu.roll(along_z, 1, 0)
            shifted_ref[3 + c, x] = along_z
            shifted_ref[6 + c, x] = pltpu.roll(along_z, ROWS - 1, 0)


def product(weight, shifted_ref, x, begin, end):
    total = None
    for a in range(3):
        for k in range(9):
            term = weight(9 * a + k) * shifted_ref[k, x + a, begin:end]
            total = term if total is None else total + term
    return total


def sweep(halo, side_ref, inverse_ref, values_ref, shifted_ref, factor, reach):
    main_ref, edge_ref, low_ref, high_ref = halo
    shifted_planes(values_ref, shifted_ref, 2 - reach, 10 + 2 * reach)

    def update(weight, x, begin, end):
        rest = side_ref[x, begin:end] - product(weight, shifted_ref, x, begin, end)
        old = values_ref[x + 1, begin:end]
        values_ref[x + 1, begin:end] = old + factor * rest * inverse_ref[x, begin:end]

    for x in range(2 - reach, 2):
        update(lambda o: low_ref[2 * o + x], x, 0, ROWS)
    for x in range(10, 10 + reach):
        update(lambda o: high_ref[2 * o + x - 10], x, 0, ROWS)

    @pl.loop(0, 8, unroll=2)
    def _(x):
        update(lambda o: main_ref[o, x], x + 2, 0, 32)
        if reach:
            update(lambda o: edge_ref[8 * o + x], x + 2, 32, ROWS)


def pre_kernel(
    steps_ref, main_ref, edge_ref, low_ref, high_ref, side_main_ref, start_ref, edge_start_ref,
    smooth_ref, residue_ref, side_ref, inverse_ref, values_ref, shifted_ref,
):
    def inverse(center):
        return jnp.where(center > 0, 1.0 / jnp.where(center > 0, center, 1.0), 0.0)

    scale = steps_ref[0]
    for x in range(2):
        side_ref[x] = low_ref[54 + x]
        side_ref[10 + x] = high_ref[54 + x]
        inverse_ref[x] = inverse(low_ref[26 + x])
        inverse_ref[10 + x] = inverse(high_ref[26 + x])
    for x in range(8):
        side_ref[2 + x, :32] = side_main_ref[x]
        side_ref[2 + x, 32:] = edge_ref[216 + x]
        inverse_ref[2 + x, :32] = inverse(main_ref[13, x])
        inverse_ref[2 + x, 32:] = inverse(edge_ref[104 + x])
        values_ref[3 + x, :32] = scale * start_ref[x]
        values_ref[3 + x, 32:] = scale * edge_start_ref[x]
    for x in range(3):
        values_ref[x] = scale * low_ref[56 + x]
        values_ref[11 + x] = scale * high_ref[56 + x]
    halo = main_ref, edge_ref, low_ref, high_ref
    sweep(halo, side_ref, inverse_ref, values_ref, shifted_ref, steps_ref[1], 2)
    sweep(halo, side_ref, inverse_ref, values_ref, shifted_ref, steps_ref[2], 1)
    shifted_planes(values_ref, shifted_ref, 2, 10)

    @pl.loop(0, 8)
    def _(x):
        smooth_ref[x] = values_ref[x + 3, :32]
        residue_ref[x] = side_main_ref[x] - product(lambda o: main_ref[o, x], shifted_ref, x + 2, 0, 32)


def stencil_scratch():
    return [pltpu.VMEM((14, ROWS, 128), F32), pltpu.VMEM((9, 14, ROWS, 128), F32)]


def pre_smooth(steps, weights, edge, low, high, side, start, edge_start):
    cells = jax.ShapeDtypeStruct((8, 32, 128), F32)
    outside = jax.ShapeDtypeStruct((12, ROWS, 128), F32)
    vmem = pl.BlockSpec(memory_space=pltpu.VMEM)
    return pl.pallas_call(
        pre_kernel,
        out_shape=(cells, cells, outside, outside),
        in_specs=[pl.BlockSpec(memory_space=pltpu.SMEM)] + [vmem] * 7,
        scratch_shapes=stencil_scratch(),
        compiler_params=pltpu.CompilerParams(vmem_limit_bytes=16 * 2**20),
    )(steps, weights, edge, low, high, side, start, edge_start)


def post_kernel(
    steps_ref, main_ref, edge_ref, low_ref, high_ref, side_ref, inverse_ref,
    cells_ref, below_ref, beyond_ref, left_ref, right_ref,
    out_ref, values_ref, shifted_ref,
):
    values_ref[:, 32:40] = jnp.zeros((14, 8, 128), F32)
    for x in range(3):
        values_ref[x, :32] = below_ref[x]
        values_ref[11 + x, :32] = beyond_ref[x]
    for x in range(8):
        values_ref[3 + x, :32] = cells_ref[x]
    for x in range(14):
        values_ref[x, 32:35] = right_ref[x]
        values_ref[x, 37:40] = left_ref[x]
    halo = main_ref, edge_ref, low_ref, high_ref
    sweep(halo, side_ref, inverse_ref, values_ref, shifted_ref, steps_ref[3], 2)
    sweep(halo, side_ref, inverse_ref, values_ref, shifted_ref, steps_ref[4], 1)
    sweep(halo, side_ref, inverse_ref, values_ref, shifted_ref, steps_ref[5], 0)
    out_ref[...] = values_ref[3:11, :32]


def post_smooth(steps, weights, edge, low, high, side, inverse, cells, below, beyond, left, right):
    vmem = pl.BlockSpec(memory_space=pltpu.VMEM)
    return pl.pallas_call(
        post_kernel,
        out_shape=jax.ShapeDtypeStruct((8, 32, 128), F32),
        in_specs=[pl.BlockSpec(memory_space=pltpu.SMEM)] + [vmem] * 11,
        scratch_shapes=stencil_scratch(),
        compiler_params=pltpu.CompilerParams(vmem_limit_bytes=16 * 2**20),
    )(steps, weights, edge, low, high, side, inverse, cells, below, beyond, left, right)


def from_sides(axis, to_next, to_previous):
    count = lax.axis_size(axis)
    forward = [(i, i + 1) for i in range(count - 1)]
    backward = [(target, source) for source, target in forward]
    return lax.ppermute(to_next, axis, forward), lax.ppermute(to_previous, axis, backward)


def halo_values(values):
    low, high = from_sides("slab", values[5:], values[:3])

    def rows(first):
        return jnp.concatenate(
            [low[:, first : first + 3], values[:, first : first + 3], high[:, first : first + 3]],
            axis=0,
        )

    left, right = from_sides("col", rows(29), rows(0))
    return low, high, left, right


def shards(
    right_side, stencil_weights, cheb_steps, send_slot, recv_index, coarse_diag, coarse_lower
):
    me = lax.axis_index("slab")
    index = recv_index[0, 0]
    place = jnp.reshape(me, (1,)).astype(jnp.int32)
    blocks = own_blocks(place, coarse_diag[0, 0], coarse_lower[0, 0], index)
    every = lax.all_gather(blocks[None], "slab", axis=0, tiled=True)

    to_next, to_previous, start = cut(stencil_weights, right_side)
    left, right = from_sides("col", to_next, to_previous)
    to_next, to_previous, edge, edge_start = pack(stencil_weights, right_side, start, left, right)
    low, high = from_sides("slab", to_next, to_previous)
    smooth, residue, side, inverse_center = pre_smooth(
        cheb_steps, stencil_weights, edge, low, high, right_side, start, edge_start
    )
    slot = send_slot.reshape(-1, 128)
    sums = scatter(slot, residue.reshape(-1, 128))
    arrived = lax.all_to_all(sums, "slab", split_axis=0, concat_axis=0, tiled=True)
    mine_rhs = collect(index, arrived)
    rhs = lax.all_to_all(mine_rhs, "slab", split_axis=0, concat_axis=0, tiled=True)

    table = jnp.concatenate(
        [
            lax.dynamic_index_in_dim(every, 256 + me, 1, False),
            lax.dynamic_index_in_dim(every, 288 + me, 1, False),
        ]
    )
    unknown = lookup(slot, table)
    coarse_x = solve(factor(every), rhs)
    corrected = gather(slot, unknown, coarse_x, smooth)
    return post_smooth(
        cheb_steps, stencil_weights, edge, low, high, side, inverse_center,
        corrected, *halo_values(corrected),
    )


def solution(mesh):
    placed = (
        P("slab", "col", None),
        P(None, "slab", "col", None),
        P(),
        P("slab", "col", None),
        P("slab", "col", None, None),
        P("slab", "col", None, None),
        P("slab", "col", None, None),
    )
    return jax.shard_map(
        shards, mesh=mesh, in_specs=placed, out_specs=P("slab", "col", None), check_vma=False
    )
```

```python
import functools

import jax
import jax.numpy as jnp
from jax import lax
from jax.experimental import pallas as pl
from jax.experimental.pallas import tpu as pltpu
from jax.sharding import PartitionSpec as P

F32 = jnp.float32
BF16 = jnp.bfloat16
ROWS = 40
SMOOTH = 3


def nn(a, b):
    return lax.dot_general(a, b, (((1,), (0,)), ((), ())), preferred_element_type=F32)

def nt(a, b):
    return lax.dot_general(a, b, (((1,), (1,)), ((), ())), preferred_element_type=F32)

def split(a):
    high = a.astype(BF16)
    return high, (a - high.astype(F32)).astype(BF16)

def one_hot(index_row, size):
    width = index_row.shape[1]
    wide = jnp.broadcast_to(index_row.astype(F32), (size, width)).astype(BF16)
    rows = lax.broadcasted_iota(jnp.int32, (size, width), 0).astype(F32).astype(BF16)
    return jnp.where(rows == wide, jnp.bfloat16(1), jnp.bfloat16(0))

def pair(block, first):
    return jnp.concatenate([block[first : first + 1], block[first + 1 : first + 2]], axis=1)

def gather_rows(table, height, parts, high, low):
    rows = []
    for first in range(0, 8, 2):
        picked = nn(table, one_hot(pair(low, first), 128))
        value = picked[:height]
        for part in range(1, parts):
            value = value + picked[part * height : (part + 1) * height]
        mask = lax.broadcasted_iota(jnp.int32, (height, 256), 0) == pair(high, first)
        row = jnp.sum(jnp.where(mask, value, 0.0), axis=0, keepdims=True)
        rows += [row[:, :128], row[:, 128:]]
    return jnp.concatenate(rows, axis=0)

def slot_row(slot):
    return ((slot >> 7) & 1) * 32 + (slot >> 8)


def lookup_kernel(place_ref, slot_ref, every_ref, out_ref, table_ref):
    me = place_ref[0]
    for owner in range(32):
        table_ref[owner : owner + 1] = every_ref[owner, pl.ds(256 + me, 1)]
        table_ref[32 + owner : 33 + owner] = every_ref[owner, pl.ds(288 + me, 1)]
    table = table_ref[...].astype(BF16)

    @pl.loop(0, slot_ref.shape[0] // 8, unroll=8)
    def _(block):
        where = pl.ds(pl.multiple_of(block * 8, 8), 8)
        slot = slot_ref[where]
        found = gather_rows(table, 64, 1, slot_row(slot), slot & 127)
        out_ref[where] = found.astype(jnp.int32)


def lookup(place, slot, every):
    vmem = pl.BlockSpec(memory_space=pltpu.VMEM)
    return pl.pallas_call(
        lookup_kernel,
        out_shape=jax.ShapeDtypeStruct(slot.shape, jnp.int32),
        in_specs=[pl.BlockSpec(memory_space=pltpu.SMEM), vmem, vmem],
        scratch_shapes=[pltpu.VMEM((64, 128), F32)],
        compiler_params=pltpu.CompilerParams(vmem_limit_bytes=12 * 2**20),
    )(place, slot, every)


def scatter_kernel(slot_ref, value_ref, out_ref):
    def step(block, total):
        where = pl.ds(pl.multiple_of(block * 8, 8), 8)
        slot = slot_ref[where]
        high_slot, low_slot = slot_row(slot), slot & 127
        value = value_ref[where]
        value_high = value.astype(BF16).astype(F32)
        value_low = value - value_high
        for first in range(0, 8, 2):
            mask = lax.broadcasted_iota(jnp.int32, (64, 256), 0) == pair(high_slot, first)
            high = jnp.where(mask, pair(value_high, first), 0.0).astype(BF16)
            low = jnp.where(mask, pair(value_low, first), 0.0).astype(BF16)
            total = total + nt(jnp.concatenate([high, low], axis=0), one_hot(pair(low_slot, first), 128))
        return total

    total = lax.fori_loop(0, slot_ref.shape[0] // 8, step, jnp.zeros((128, 128), F32), unroll=8)
    total = total[:64] + total[64:]
    out_ref[...] = jnp.concatenate([total[:32], total[32:]], axis=1)


def scatter(slot, value):
    return pl.pallas_call(
        scatter_kernel,
        out_shape=jax.ShapeDtypeStruct((32, 256), F32),
        compiler_params=pltpu.CompilerParams(vmem_limit_bytes=8 * 2**20),
    )(slot, value)


def collect_kernel(index_ref, value_ref, out_ref):
    total = jnp.zeros((16, 128), F32)
    for source in range(32):
        row = value_ref[source : source + 1]
        high, low = split(jnp.concatenate([row] * 8, axis=0))
        spread = jnp.concatenate([high, low], axis=0)
        total = total + nt(spread, one_hot(index_ref[source : source + 1], 128))
    row = total[0:1] + total[8:9]
    out_ref[...] = jnp.concatenate([row] * 32, axis=0)


def collect(index, value):
    return pl.pallas_call(
        collect_kernel,
        out_shape=jax.ShapeDtypeStruct((32, 128), F32),
        compiler_params=pltpu.CompilerParams(vmem_limit_bytes=8 * 2**20),
    )(index, value)


def gather_kernel(slot_ref, unknown_ref, table_ref, base_ref, out_ref):
    high, low = split(table_ref[...])
    table = jnp.concatenate([high, low], axis=0)

    @pl.loop(0, slot_ref.shape[0] // 8, unroll=8)
    def _(block):
        where = pl.ds(pl.multiple_of(block * 8, 8), 8)
        rows = pl.ds(pl.multiple_of((block % 4) * 8, 8), 8)
        found = gather_rows(table, 32, 2, slot_ref[where] >> 8, unknown_ref[where])
        out_ref[block // 4, rows] = base_ref[block // 4, rows] + found


def gather(slot, unknown, table, base):
    return pl.pallas_call(
        gather_kernel,
        out_shape=jax.ShapeDtypeStruct(base.shape, F32),
        compiler_params=pltpu.CompilerParams(vmem_limit_bytes=8 * 2**20),
    )(slot, unknown, table, base)


def mm3(form, a, b):
    ah, al = split(a)
    bh, bl = split(b)
    return form(ah, bh) + (form(ah, bl) + form(al, bh))

def mm1(a, b):
    return nn(a.astype(BF16), b.astype(BF16))

def norm1(e):
    return jnp.max(jnp.sum(jnp.abs(e), axis=0, keepdims=True))

def invert(count, get_a, x_ref, r_ref):
    n = 128
    rows = lax.broadcasted_iota(jnp.int32, (n, n), 0)
    cols = lax.broadcasted_iota(jnp.int32, (n, n), 1)
    eye = (rows == cols).astype(F32)

    def recip_row(a):
        return 1.0 / jnp.sum(a * eye, axis=0, keepdims=True)

    rho = jnp.float32(0)
    for b in range(count):
        a = get_a(b)
        r = eye - a * recip_row(a)
        r_ref[b] = r
        x_ref[b] = eye + r
        rho = jnp.maximum(rho, norm1(r))

    def square_cond(state):
        bound, steps = state
        return jnp.logical_and(bound > 2e-3, steps < 20)

    def square(state):
        bound, steps = state
        for b in range(count):
            r = r_ref[b].astype(BF16)
            r2 = nn(r, r)
            y = x_ref[b]
            r_ref[b] = r2
            x_ref[b] = y + nn(y.astype(BF16), r2.astype(BF16))
        return bound * bound, steps + 1

    lax.while_loop(square_cond, square, (rho, jnp.int32(0)))

    def residual():
        worst = jnp.float32(0)
        for b in range(count):
            e = eye - mm3(nn, get_a(b), x_ref[b])
            r_ref[b] = e
            worst = jnp.maximum(worst, norm1(e))
        return worst

    def correct():
        for b in range(count):
            x = x_ref[b]
            x_ref[b] = x + mm3(nn, x, r_ref[b])

    for b in range(count):
        d = recip_row(get_a(b))
        dcol = jnp.sum(eye * d, axis=1, keepdims=True)
        x_ref[b] = x_ref[b] * dcol
    first = residual()

    def restart():
        for b in range(count):
            a = get_a(b)
            x_ref[b] = eye * recip_row(a)
        return residual()

    first = lax.cond(first < 0.5, lambda: first, restart)

    def newton_cond(state):
        worst, steps = state
        return jnp.logical_and(worst > 2e-3, steps < 60)

    def newton(state):
        correct()
        return residual(), state[1] + 1

    lax.while_loop(newton_cond, newton, (first, jnp.int32(0)))
    correct()

def blocks_kernel(place_ref, diag_ref, lower_ref, index_ref, out_ref, x_ref, r_ref):
    invert(1, lambda b: diag_ref[...], x_ref, r_ref)
    odd = place_ref[0] % 2 == 1
    out_ref[0:128] = jnp.where(odd, x_ref[0], diag_ref[...])
    out_ref[128:256] = lower_ref[...]
    out_ref[256:288] = index_ref[:, :128].astype(F32)
    out_ref[288:320] = index_ref[:, 128:].astype(F32)


def own_blocks(place, diag, lower, index):
    vmem = pl.BlockSpec(memory_space=pltpu.VMEM)
    return pl.pallas_call(
        blocks_kernel,
        out_shape=jax.ShapeDtypeStruct((320, 128), F32),
        in_specs=[pl.BlockSpec(memory_space=pltpu.SMEM), vmem, vmem, vmem],
        scratch_shapes=[pltpu.VMEM((1, 128, 128), F32), pltpu.VMEM((1, 128, 128), F32)],
        compiler_params=pltpu.CompilerParams(vmem_limit_bytes=4 * 2**20),
    )(place, diag, lower, index)


def row3(form, row, mat):
    rh, rl = split(row)
    mh, ml = split(mat)
    return form(rh, mh) + (form(rl, mh) + form(rh, ml))


def chain_kernel(count, every_ref, rhs_ref, out_ref, kept_ref, d_ref, l_ref, x_ref, y_ref, r_ref):
    stride = 1
    while stride < count:
        gone = list(range(stride, count, 2 * stride))
        src_d = every_ref.at[:, 0:128] if stride == 1 else d_ref
        src_l = every_ref.at[:, 128:256] if stride == 1 else l_ref
        if stride > 1:
            invert(len(gone), lambda b: src_d[gone[b]], x_ref, y_ref)
        for b, j in enumerate(gone):
            inverse = src_d[j] if stride == 1 else x_ref[b]
            kept_ref[j, 0:128] = inverse
            kept_ref[j, 128:256] = mm3(nn, src_l[j].T, inverse)
            if j + stride < count:
                kept_ref[j, 256:384] = mm3(nn, src_l[j + stride], inverse)
        for i in range(0, count, 2 * stride):
            high = i + stride
            value = src_d[i] - mm3(nn, kept_ref[high, 128:256], src_l[high])
            if i > 0:
                low = i - stride
                after = kept_ref[low, 256:384]
                value = value - mm3(nt, after, src_l[i])
                l_ref[i] = -mm3(nn, after, src_l[low])
            d_ref[i] = value
        stride *= 2
    invert(1, lambda b: d_ref[0], x_ref, y_ref)

    r_ref[...] = rhs_ref[...]
    stride = 1
    while stride < count:
        for j in range(stride, count, 2 * stride):
            row = r_ref[pl.ds(j, 1)]
            if j + stride < count:
                t = row3(nt, row, kept_ref[j, 128:384])
                r_ref[pl.ds(j + stride, 1)] = r_ref[pl.ds(j + stride, 1)] - t[:, 128:]
            else:
                t = row3(nt, row, kept_ref[j, 128:256])
            r_ref[pl.ds(j - stride, 1)] = r_ref[pl.ds(j - stride, 1)] - t[:, :128]
        stride *= 2
    out_ref[0:1] = row3(nn, r_ref[0:1], x_ref[0])
    while stride > 1:
        stride //= 2
        for j in range(stride, count, 2 * stride):
            x = row3(nn, r_ref[pl.ds(j, 1)], kept_ref[j, 0:128])
            x = x - row3(nn, out_ref[pl.ds(j - stride, 1)], kept_ref[j, 128:256])
            if j + stride < count:
                x = x - row3(nn, out_ref[pl.ds(j + stride, 1)], kept_ref[j, 256:384])
            out_ref[pl.ds(j, 1)] = x


def chain_solve(every, rhs):
    count = every.shape[0]
    return pl.pallas_call(
        functools.partial(chain_kernel, count),
        out_shape=jax.ShapeDtypeStruct((count, 128), F32),
        scratch_shapes=[
            pltpu.VMEM((count, 384, 128), F32),
            pltpu.VMEM((count, 128, 128), F32),
            pltpu.VMEM((count, 128, 128), F32),
            pltpu.VMEM((count // 4, 128, 128), F32),
            pltpu.VMEM((count // 4, 128, 128), F32),
            pltpu.VMEM((count, 128), F32),
        ],
        compiler_params=pltpu.CompilerParams(vmem_limit_bytes=24 * 2**20),
    )(every, rhs)


def cut_kernel(weights_ref, side_ref, next_ref, previous_ref, start_ref):
    for offset in range(27):
        for x in range(8):
            next_ref[8 * offset + x] = weights_ref[offset, x, 30:32]
            previous_ref[8 * offset + x] = weights_ref[offset, x, 0:2]
    for x in range(8):
        start_ref[x] = side_ref[x] / weights_ref[13, x]
        next_ref[216 + x] = side_ref[x, 30:32]
        previous_ref[216 + x] = side_ref[x, 0:2]
        next_ref[224 + x] = start_ref[x, 29:31]
        next_ref[232 + x] = start_ref[x, 30:32]
        previous_ref[224 + x] = start_ref[x, 0:2]
        previous_ref[232 + x] = start_ref[x, 1:3]


def cut(weights, side):
    rows = jax.ShapeDtypeStruct((240, 2, 128), F32)
    return pl.pallas_call(
        cut_kernel,
        out_shape=(rows, rows, jax.ShapeDtypeStruct((8, 32, 128), F32)),
        compiler_params=pltpu.CompilerParams(vmem_limit_bytes=10 * 2**20),
    )(weights, side)


def pack_kernel(
    weights_ref, side_ref, start_ref, left_ref, right_ref,
    next_ref, previous_ref, edge_ref, edge_start_ref,
):
    edge_ref[...] = jnp.zeros((224, 8, 128), F32)
    edge_start_ref[...] = jnp.zeros((8, 8, 128), F32)

    @pl.loop(0, 224)
    def _(k):
        edge_ref[k, 0:2] = right_ref[k]
        edge_ref[k, 6:8] = left_ref[k]

    for x in range(8):
        edge_start_ref[x, 0:2] = right_ref[224 + x]
        edge_start_ref[x, 1:3] = right_ref[232 + x]
        edge_start_ref[x, 5:7] = left_ref[224 + x]
        edge_start_ref[x, 6:8] = left_ref[232 + x]

    @pl.loop(0, 27)
    def _(offset):
        for x in range(2):
            next_ref[2 * offset + x, :32] = weights_ref[offset, 6 + x]
            next_ref[2 * offset + x, 32:] = edge_ref[8 * offset + 6 + x]
            previous_ref[2 * offset + x, :32] = weights_ref[offset, x]
            previous_ref[2 * offset + x, 32:] = edge_ref[8 * offset + x]

    for x in range(2):
        next_ref[54 + x, :32] = side_ref[6 + x]
        next_ref[54 + x, 32:] = edge_ref[222 + x]
        previous_ref[54 + x, :32] = side_ref[x]
        previous_ref[54 + x, 32:] = edge_ref[216 + x]
    for x in range(3):
        next_ref[56 + x, :32] = start_ref[5 + x]
        next_ref[56 + x, 32:] = edge_start_ref[5 + x]
        previous_ref[56 + x, :32] = start_ref[x]
        previous_ref[56 + x, 32:] = edge_start_ref[x]


def pack(weights, side, start, left, right):
    planes = jax.ShapeDtypeStruct((59, ROWS, 128), F32)
    return pl.pallas_call(
        pack_kernel,
        out_shape=(
            planes, planes,
            jax.ShapeDtypeStruct((224, 8, 128), F32), jax.ShapeDtypeStruct((8, 8, 128), F32),
        ),
        compiler_params=pltpu.CompilerParams(vmem_limit_bytes=16 * 2**20),
    )(weights, side, start, left, right)


def shifted_planes(values_ref, shifted_ref, first, count):
    lane = lax.broadcasted_iota(jnp.int32, (ROWS, 128), 1)

    @pl.loop(first, first + count, unroll=2)
    def _(x):
        plane = values_ref[x]
        below = jnp.where(lane == 0, 0.0, pltpu.roll(plane, 1, 1))
        above = jnp.where(lane == 127, 0.0, pltpu.roll(plane, 127, 1))
        for c, along_z in enumerate((below, plane, above)):
            shifted_ref[c, x] = pltpu.roll(along_z, 1, 0)
            shifted_ref[3 + c, x] = along_z
            shifted_ref[6 + c, x] = pltpu.roll(along_z, ROWS - 1, 0)


def product(weight, shifted_ref, x, begin, end):
    total = None
    for a in range(3):
        for k in range(9):
            term = weight(9 * a + k) * shifted_ref[k, x + a, begin:end]
            total = term if total is None else total + term
    return total


def sweep(halo, side_ref, inverse_ref, values_ref, shifted_ref, factor, reach):
    main_ref, edge_ref, low_ref, high_ref = halo
    shifted_planes(values_ref, shifted_ref, 2 - reach, 10 + 2 * reach)

    def update(weight, x, begin, end):
        rest = side_ref[x, begin:end] - product(weight, shifted_ref, x, begin, end)
        old = values_ref[x + 1, begin:end]
        values_ref[x + 1, begin:end] = old + factor * rest * inverse_ref[x, begin:end]

    for x in range(2 - reach, 2):
        update(lambda o: low_ref[2 * o + x], x, 0, ROWS)
    for x in range(10, 10 + reach):
        update(lambda o: high_ref[2 * o + x - 10], x, 0, ROWS)

    @pl.loop(0, 8, unroll=2)
    def _(x):
        update(lambda o: main_ref[o, x], x + 2, 0, 32)
        if reach:
            update(lambda o: edge_ref[8 * o + x], x + 2, 32, ROWS)


def pre_kernel(
    steps_ref, main_ref, edge_ref, low_ref, high_ref, side_main_ref, start_ref, edge_start_ref,
    smooth_ref, residue_ref, side_ref, inverse_ref, values_ref, shifted_ref,
):
    def inverse(center):
        return jnp.where(center > 0, 1.0 / jnp.where(center > 0, center, 1.0), 0.0)

    scale = steps_ref[0]
    for x in range(2):
        side_ref[x] = low_ref[54 + x]
        side_ref[10 + x] = high_ref[54 + x]
        inverse_ref[x] = inverse(low_ref[26 + x])
        inverse_ref[10 + x] = inverse(high_ref[26 + x])
    for x in range(8):
        side_ref[2 + x, :32] = side_main_ref[x]
        side_ref[2 + x, 32:] = edge_ref[216 + x]
        inverse_ref[2 + x, :32] = inverse(main_ref[13, x])
        inverse_ref[2 + x, 32:] = inverse(edge_ref[104 + x])
        values_ref[3 + x, :32] = scale * start_ref[x]
        values_ref[3 + x, 32:] = scale * edge_start_ref[x]
    for x in range(3):
        values_ref[x] = scale * low_ref[56 + x]
        values_ref[11 + x] = scale * high_ref[56 + x]
    halo = main_ref, edge_ref, low_ref, high_ref
    sweep(halo, side_ref, inverse_ref, values_ref, shifted_ref, steps_ref[1], 2)
    sweep(halo, side_ref, inverse_ref, values_ref, shifted_ref, steps_ref[2], 1)
    shifted_planes(values_ref, shifted_ref, 2, 10)

    @pl.loop(0, 8)
    def _(x):
        smooth_ref[x] = values_ref[x + 3, :32]
        residue_ref[x] = side_main_ref[x] - product(lambda o: main_ref[o, x], shifted_ref, x + 2, 0, 32)


def stencil_scratch():
    return [pltpu.VMEM((14, ROWS, 128), F32), pltpu.VMEM((9, 14, ROWS, 128), F32)]


def pre_smooth(steps, weights, edge, low, high, side, start, edge_start):
    cells = jax.ShapeDtypeStruct((8, 32, 128), F32)
    outside = jax.ShapeDtypeStruct((12, ROWS, 128), F32)
    vmem = pl.BlockSpec(memory_space=pltpu.VMEM)
    return pl.pallas_call(
        pre_kernel,
        out_shape=(cells, cells, outside, outside),
        in_specs=[pl.BlockSpec(memory_space=pltpu.SMEM)] + [vmem] * 7,
        scratch_shapes=stencil_scratch(),
        compiler_params=pltpu.CompilerParams(vmem_limit_bytes=16 * 2**20),
    )(steps, weights, edge, low, high, side, start, edge_start)


def post_kernel(
    steps_ref, main_ref, edge_ref, low_ref, high_ref, side_ref, inverse_ref,
    cells_ref, below_ref, beyond_ref, left_ref, right_ref,
    out_ref, values_ref, shifted_ref,
):
    values_ref[:, 32:40] = jnp.zeros((14, 8, 128), F32)
    for x in range(3):
        values_ref[x, :32] = below_ref[x]
        values_ref[11 + x, :32] = beyond_ref[x]
    for x in range(8):
        values_ref[3 + x, :32] = cells_ref[x]
    for x in range(14):
        values_ref[x, 32:35] = right_ref[x]
        values_ref[x, 37:40] = left_ref[x]
    halo = main_ref, edge_ref, low_ref, high_ref
    sweep(halo, side_ref, inverse_ref, values_ref, shifted_ref, steps_ref[3], 2)
    sweep(halo, side_ref, inverse_ref, values_ref, shifted_ref, steps_ref[4], 1)
    sweep(halo, side_ref, inverse_ref, values_ref, shifted_ref, steps_ref[5], 0)
    out_ref[...] = values_ref[3:11, :32]


def post_smooth(steps, weights, edge, low, high, side, inverse, cells, below, beyond, left, right):
    vmem = pl.BlockSpec(memory_space=pltpu.VMEM)
    return pl.pallas_call(
        post_kernel,
        out_shape=jax.ShapeDtypeStruct((8, 32, 128), F32),
        in_specs=[pl.BlockSpec(memory_space=pltpu.SMEM)] + [vmem] * 11,
        scratch_shapes=stencil_scratch(),
        compiler_params=pltpu.CompilerParams(vmem_limit_bytes=16 * 2**20),
    )(steps, weights, edge, low, high, side, inverse, cells, below, beyond, left, right)


def from_sides(axis, to_next, to_previous):
    count = lax.axis_size(axis)
    forward = [(i, i + 1) for i in range(count - 1)]
    backward = [(target, source) for source, target in forward]
    return lax.ppermute(to_next, axis, forward), lax.ppermute(to_previous, axis, backward)


def halo_values(values):
    low, high = from_sides("slab", values[5:], values[:3])

    def rows(first):
        return jnp.concatenate(
            [low[:, first : first + 3], values[:, first : first + 3], high[:, first : first + 3]],
            axis=0,
        )

    left, right = from_sides("col", rows(29), rows(0))
    return low, high, left, right


def shards(
    right_side, stencil_weights, cheb_steps, send_slot, recv_index, coarse_diag, coarse_lower
):
    me = lax.axis_index("slab")
    index = recv_index[0, 0]
    place = jnp.reshape(me, (1,)).astype(jnp.int32)
    blocks = own_blocks(place, coarse_diag[0, 0], coarse_lower[0, 0], index)
    every = lax.all_gather(blocks[None], "slab", axis=0, tiled=True)

    to_next, to_previous, start = cut(stencil_weights, right_side)
    left, right = from_sides("col", to_next, to_previous)
    to_next, to_previous, edge, edge_start = pack(stencil_weights, right_side, start, left, right)
    low, high = from_sides("slab", to_next, to_previous)
    smooth, residue, side, inverse_center = pre_smooth(
        cheb_steps, stencil_weights, edge, low, high, right_side, start, edge_start
    )
    slot = send_slot.reshape(-1, 128)
    sums = scatter(slot, residue.reshape(-1, 128))
    arrived = lax.all_to_all(sums, "slab", split_axis=0, concat_axis=0, tiled=True)
    mine_rhs = collect(index, arrived)
    rhs = lax.all_to_all(mine_rhs, "slab", split_axis=0, concat_axis=0, tiled=True)

    unknown = lookup(place, slot, every)
    coarse_x = chain_solve(every, rhs)
    corrected = gather(slot, unknown, coarse_x, smooth)
    return post_smooth(
        cheb_steps, stencil_weights, edge, low, high, side, inverse_center,
        corrected, *halo_values(corrected),
    )


def solution(mesh):
    placed = (
        P("slab", "col", None),
        P(None, "slab", "col", None),
        P(),
        P("slab", "col", None),
        P("slab", "col", None, None),
        P("slab", "col", None, None),
        P("slab", "col", None, None),
    )
    return jax.shard_map(
        shards, mesh=mesh, in_specs=placed, out_specs=P("slab", "col", None), check_vma=False
    )
```
